512 devices in a mesh: aa: 32 (over x, z_lo, core), ba: 16 (over y, z_hi).
Axes of the slice: x: 4, y: 4, z: 16 (z_hi: 4, z_lo: 4; z = z_hi * 4 + z_lo), core: 2. Of those that a mesh axis runs over, the one named last changes fastest.
Arguments:
- amplitudes: bfloat16 [1024, 2048], P('ba', 'aa'), may hold values from -6 to 6
- integrals: bfloat16 [512, 512, 2048], P('aa', 'ba'), may hold values from -0.125 to 0.125
- virt_energy: float32 [512], replicated, may hold values from 0.2 to 2
- pair_energy: float32 [1024], replicated, may hold values from 0.3 to 3
Outputs:
- update: float32 [512, 512, 1024], P('aa', 'ba')
The draws below stay inside these ranges and needn't reach their ends.
All inputs are finite; a program needn't handle non-finite values.
Results may differ from the reference program's by a relative error of at most 0.0003.
Values may be sent and summed in bfloat16 or wider, within the bound.
No kernel may reach another device: no remote copies, remote signals or barrier semaphores. Data moves between devices by JAX's collectives and lax.ppermute only.
A program may use at most 64 MiB of HBM per device.

```python
import math
import jax
import jax.numpy as jnp
from jax import lax

NV = 512
K = 2048
P_SIZE = 1024


def steps_of(own_key, shape, split, low, high):
    gain, own = 1.0, jax.random.fold_in(own_key, 6)
    for axis_at, blocks in split:
        draws = jnp.exp(jax.random.uniform(jax.random.fold_in(own, axis_at), (blocks,), jnp.float32, low / len(split), high / len(split)))
        gain = gain * jnp.repeat(draws, shape[axis_at] // blocks).reshape([-1 if axis == axis_at else 1 for axis in range(len(shape))])
    return gain


def scatter_about(rng, extent, deviation, bound, split=(), kind=jnp.bfloat16):
    result = jax.random.normal(rng, extent, jnp.float32) * deviation
    if len(split) > 0:
        result = steps_of(rng, extent, split, -0.22, 0.18) * result
    return jnp.clip(result, min=-bound, max=bound).astype(kind)


def setup_inputs(seed: int = 0) -> dict:
    key_of = jax.random.split(jax.random.key(seed), 5)
    return {
        "amplitudes": scatter_about(key_of[0], (P_SIZE, K), 1.0, 6.0, ((0, 16), (1, 32))),
        "integrals": scatter_about(key_of[1], (NV, NV, K), K ** -0.5, 0.125, ((0, 32), (1, 16))),
        "virt_energy": jnp.clip(jnp.exp(jax.random.uniform(key_of[2], (NV,), jnp.float32, math.log(0.2), math.log(2.0))), 0.2, 2.0),
        "pair_energy": jnp.clip(jnp.exp(jax.random.uniform(key_of[3], (P_SIZE,), jnp.float32, math.log(0.3), math.log(3.0))), 0.3, 3.0),
    }


def reference(amplitudes, integrals, virt_energy, pair_energy):
    flat = integrals.reshape(NV * NV, K)
    ladder = lax.dot_general(flat, amplitudes, (((1,), (1,)), ((), ())), preferred_element_type=jnp.float32)
    ladder = ladder.reshape(NV, NV, P_SIZE)
    denom = virt_energy[:, None, None] + virt_energy[None, :, None] + pair_energy[None, None, :]
    return ladder / denom
```

```python
import functools

import jax
import jax.numpy as jnp
from jax import lax
from jax.experimental import pallas as pl
from jax.experimental.pallas import tpu as pltpu
from jax.sharding import PartitionSpec as P

AXES = ("aa", "ba")
SIDE = 4
DEPTH = 16


def flat(x, y, z, core):
    z_hi, z_lo = divmod(z % DEPTH, SIDE)
    return (((x % SIDE) * SIDE + z_lo) * 2 + core) * DEPTH + (y % SIDE) * SIDE + z_hi


def z_groups():
    return [
        [flat(x, y, z, core) for z in range(DEPTH)]
        for x in range(SIDE) for y in range(SIDE) for core in range(2)
    ]


def plane_groups(x_core):
    return [
        [flat(i, u, z, core) if core == x_core else flat(u, i, z, core) for i in range(SIDE)]
        for u in range(SIDE) for z in range(DEPTH) for core in range(2)
    ]


def gather(block, groups):
    count = len(groups[0])
    sent = jnp.broadcast_to(block[None], (count, *block.shape))
    return lax.all_to_all(sent, AXES, 0, 0, axis_index_groups=groups, tiled=True)


def ladder_kernel(place_ref, ints_ref, own_ref, other_ref, energy_ref, pair_ref, out_ref, amps_ref):
    core = place_ref[0]
    lane = lax.broadcasted_iota(jnp.int32, (32, 128), 1)
    own_first = (lane < 64) == (core == 0)
    for y in range(SIDE):
        for x in range(SIDE):
            i = jnp.where(core == 0, y, x)
            j = jnp.where(core == 0, x, y)
            for z in range(DEPTH):
                own = own_ref[i, j, z]
                other = other_ref[j, i, z]
                z_hi, z_lo = divmod(z, SIDE)
                row = (y * SIDE + z_hi) * 64
                column = (x * SIDE + z_lo) * 128
                amps_ref[row : row + 32, column : column + 128] = jnp.where(own_first, own, other)
                swapped = jnp.where(own_first, other, own)
                amps_ref[row + 32 : row + 64, column : column + 128] = pltpu.roll(swapped, 64, 1)
    for n in range(0, 1024, 256):
        ladder = lax.dot_general(
            ints_ref[...], amps_ref[n : n + 256, :], (((1,), (1,)), ((), ())),
            preferred_element_type=jnp.float32,
        )
        out_ref[:, n : n + 256] = ladder / (energy_ref[...] + pair_ref[:, n : n + 256])


def on_device(amplitudes, integrals, virt_energy, pair_energy):
    first_count, second_count, cd_count = integrals.shape
    core = lax.rem(lax.axis_index("aa"), 2)
    upper, lower = amplitudes[:32], amplitudes[32:]
    left = jnp.where(core == 0, upper, lower)
    right = jnp.where(core == 0, lower, upper)
    block = jnp.concatenate([left, right], axis=1)
    block = gather(block, z_groups()).reshape(1, DEPTH * 32, 128)[0]
    block = gather(block, plane_groups(0)).reshape(SIDE * DEPTH * 32, 128)
    own = gather(block, plane_groups(1)).reshape(SIDE, SIDE, DEPTH, 32, 128)
    across = [(i, i ^ 1) for i in range(lax.axis_size("aa"))]
    other = lax.ppermute(own, "aa", across)

    first_energy = lax.dynamic_slice_in_dim(
        virt_energy, lax.axis_index("aa") * first_count, first_count, 0
    )
    second_energy = lax.dynamic_slice_in_dim(
        virt_energy, lax.axis_index("ba") * second_count, second_count, 0
    )
    energy = (first_energy[:, None] + second_energy[None, :]).reshape(-1, 1)
    rows, pairs = first_count * second_count, pair_energy.shape[0]
    vmem = pl.BlockSpec(memory_space=pltpu.VMEM)
    update = pl.pallas_call(
        ladder_kernel,
        out_shape=jax.ShapeDtypeStruct((rows, pairs), jnp.float32),
        in_specs=[pl.BlockSpec(memory_space=pltpu.SMEM)] + [vmem] * 5,
        out_specs=vmem,
        scratch_shapes=[pltpu.VMEM((pairs, cd_count), jnp.bfloat16)],
        compiler_params=pltpu.CompilerParams(vmem_limit_bytes=40 * 2**20),
        cost_estimate=pl.CostEstimate(flops=2 * rows * pairs * cd_count, bytes_accessed=2**23, transcendentals=0),
    )(
        core.reshape(1).astype(jnp.int32), integrals.reshape(rows, cd_count), own, other,
        energy, pair_energy.reshape(1, -1),
    )
    return update.reshape(first_count, second_count, pairs)


def solution(mesh):
    placed = (P("ba", "aa"), P("aa", "ba", None), P(), P())
    return jax.shard_map(
        on_device, mesh=mesh, in_specs=placed, out_specs=P("aa", "ba", None), check_vma=False
    )
```

```python
import functools

import jax
import jax.numpy as jnp
from jax import lax
from jax.experimental import pallas as pl
from jax.experimental.pallas import tpu as pltpu
from jax.sharding import PartitionSpec as P

AXES = ("aa", "ba")
SIDE = 4
DEPTH = 16
FIRSTS, SECONDS = 16, 32
TILE = 256


def flat(x, y, z, core):
    z_hi, z_lo = divmod(z % DEPTH, SIDE)
    return (((x % SIDE) * SIDE + z_lo) * 2 + core) * DEPTH + (y % SIDE) * SIDE + z_hi


def everywhere():
    return [
        (x, y, z, core)
        for x in range(SIDE) for y in range(SIDE) for z in range(DEPTH) for core in range(2)
    ]


def z_groups():
    return [
        [flat(x, y, z, core) for z in range(DEPTH)]
        for x in range(SIDE) for y in range(SIDE) for core in range(2)
    ]


def first_groups():
    return [
        [flat(i, u, z, core) if core == 0 else flat(u, i, z, core) for i in range(SIDE)]
        for u in range(SIDE) for z in range(DEPTH) for core in range(2)
    ]


def second_step(step):
    return [
        (flat(x, y, z, core), flat(x, y + step, z, core) if core == 0 else flat(x + step, y, z, core))
        for x, y, z, core in everywhere()
    ]


def core_swap():
    return [(flat(x, y, z, core), flat(x, y, z, 1 - core)) for x, y, z, core in everywhere()]


def where_am_i():
    aa, ba = lax.axis_index("aa"), lax.axis_index("ba")
    return lax.rem(aa, 2), lax.div(aa, 2 * SIDE), lax.div(ba, SIDE)


def line_kernel(in_ref, out_ref):
    low = lax.broadcasted_iota(jnp.int32, (32, 128), 1) < 64
    for z_hi in range(SIDE):
        for half in range(2):
            first = in_ref[z_hi * SIDE + 2 * half]
            second = in_ref[z_hi * SIDE + 2 * half + 1]
            upper = jnp.where(low, first, pltpu.roll(second, 64, 1))
            lower = jnp.where(low, pltpu.roll(first, 64, 1), second)
            row, column = z_hi * 64, half * 128
            for copy in range(SIDE):
                out_ref[copy, row : row + 32, column : column + 128] = upper
                out_ref[copy, row + 32 : row + 64, column : column + 128] = lower


def add_tiles(total_ref, ints_ref, mine_ref, other_ref, behind):
    core, x, y = where_am_i()
    x_from = lax.rem(x + SIDE - behind, SIDE)
    y_from = lax.rem(y + SIDE - behind, SIDE)

    def add(at_y, at_x, at_core, block):
        total_ref[at_y] += lax.dot_general(
            ints_ref[at_core, at_x], block, (((1,), (1,)), ((), ())),
            preferred_element_type=jnp.float32,
        )

    zero = core == 0
    for i in range(SIDE):
        add(jnp.where(zero, y_from, i), jnp.where(zero, i, x_from), core, mine_ref[i])
        add(jnp.where(zero, i, y_from), jnp.where(zero, x_from, i), 1 - core, other_ref[i])


def begin_kernel(virt_ref, raw_ref, pair_ref, later_ref, ints_ref, scale_ref):
    low = lax.broadcasted_iota(jnp.int32, (raw_ref.shape[0], 128), 1) < 64
    for x in range(SIDE):
        for half in range(2):
            column = x * 512 + half * 256
            first = raw_ref[:, column : column + 128]
            second = raw_ref[:, column + 128 : column + 256]
            to = slice(half * 128, half * 128 + 128)
            ints_ref[0, x, :, to] = jnp.where(low, first, pltpu.roll(second, 64, 1))
            ints_ref[1, x, :, to] = jnp.where(low, pltpu.roll(first, 64, 1), second)
    first_at, second_at = lax.axis_index("aa") * FIRSTS, lax.axis_index("ba") * SECONDS
    row = lax.broadcasted_iota(jnp.int32, (SECONDS, TILE), 0)
    seconds = jnp.zeros((SECONDS, TILE), jnp.float32)
    for b in range(SECONDS):
        seconds = jnp.where(row == b, virt_ref[second_at + b], seconds)
    for y in range(SIDE):
        pair = pair_ref[:, y * TILE : (y + 1) * TILE]
        for a in range(FIRSTS):
            denominator = virt_ref[first_at + a] + seconds + pair
            scale_ref[y, a * SECONDS : (a + 1) * SECONDS] = 1.0 / denominator


def plain_kernel(in_ref, out_ref):
    out_ref[...] = in_ref[...]


def copy_kernel(in_ref, later_ref, out_ref):
    out_ref[...] = in_ref[...]


def stack_kernel(*refs):
    for i, ref in enumerate(refs[:-1]):
        refs[-1][i] = ref[...]


def middle_kernel(ints_ref, near_ref, others_ref, total_ref):
    total_ref[...] = jnp.zeros(total_ref.shape, jnp.float32)
    for i, behind in enumerate((0, 1, 3)):
        add_tiles(total_ref, ints_ref, near_ref.at[i], others_ref.at[i], behind)


def end_kernel(ints_ref, mine_ref, other_ref, scale_ref, start_ref, out_ref, total_ref):
    for y in range(SIDE):
        total_ref[y] = start_ref[y]
    add_tiles(total_ref, ints_ref, mine_ref, other_ref, 2)
    for y in range(SIDE):
        out_ref[:, y * TILE : (y + 1) * TILE] = total_ref[y] * scale_ref[y]


SMEM = pl.BlockSpec(memory_space=pltpu.SMEM)
VMEM = pl.BlockSpec(memory_space=pltpu.VMEM)
LATER = pl.BlockSpec(memory_space=pl.ANY)


def call(kernel, ins, outs, specs=None, scratch=(), tiles=0, megabytes=16):
    return pl.pallas_call(
        kernel,
        out_shape=outs,
        in_specs=specs or [VMEM] * len(ins),
        out_specs=jax.tree.map(lambda _: VMEM, outs),
        scratch_shapes=list(scratch),
        compiler_params=pltpu.CompilerParams(vmem_limit_bytes=megabytes * 2**20),
        cost_estimate=pl.CostEstimate(
            flops=tiles * 2 * 512 * TILE * TILE, bytes_accessed=2**18, transcendentals=0
        ),
    )(*ins)


def bf16(*shape):
    return jax.ShapeDtypeStruct(shape, jnp.bfloat16)


def on_device(amplitudes, integrals, virt_energy, pair_energy):
    first_count, second_count, cd_count = integrals.shape
    rows, pairs = first_count * second_count, pair_energy.shape[0]

    packed = jnp.concatenate([amplitudes[:32], amplitudes[32:]], axis=1)
    sent = jnp.broadcast_to(packed[None], (DEPTH, 32, 128))
    lines = lax.all_to_all(sent, AXES, 0, 0, axis_index_groups=z_groups(), tiled=True)
    sent = call(line_kernel, (lines,), bf16(SIDE, TILE, TILE), megabytes=4)
    mine = lax.all_to_all(sent, AXES, 0, 0, axis_index_groups=first_groups(), tiled=True)

    before = lax.ppermute(mine, AXES, second_step(1))
    after = lax.ppermute(mine, AXES, second_step(-1))
    totals = jax.ShapeDtypeStruct((SIDE, rows, TILE), jnp.float32)
    ints, scale = call(
        begin_kernel,
        (virt_energy, integrals.reshape(rows, cd_count), pair_energy.reshape(1, -1), mine),
        (bf16(2, SIDE, rows, TILE), totals),
        specs=[SMEM, VMEM, VMEM, LATER], tiles=4,
    )
    relayed = call(copy_kernel, (before, scale), bf16(SIDE, TILE, TILE), specs=[VMEM, LATER], megabytes=2)
    far = lax.ppermute(relayed, AXES, second_step(1))
    near = call(stack_kernel, (mine, before, after), bf16(3, SIDE, TILE, TILE), megabytes=4)
    others = lax.ppermute(near, AXES, core_swap())
    far = call(plain_kernel, (far,), bf16(SIDE, TILE, TILE), tiles=400, megabytes=2)
    other_far = lax.ppermute(far, AXES, core_swap())
    total = call(middle_kernel, (ints, near, others), totals, tiles=24)
    update = call(
        end_kernel,
        (ints, far, other_far, scale, total),
        jax.ShapeDtypeStruct((rows, pairs), jnp.float32),
        scratch=[pltpu.VMEM((SIDE, rows, TILE), jnp.float32)],
        tiles=8,
    )
    return update.reshape(first_count, second_count, pairs)


def solution(mesh):
    placed = (P("ba", "aa"), P("aa", "ba", None), P(), P())
    return jax.shard_map(
        on_device, mesh=mesh, in_specs=placed, out_specs=P("aa", "ba", None), check_vma=False
    )
```

```python
import jax
import jax.numpy as jnp
from jax import lax
from jax.experimental import pallas as pl
from jax.experimental.pallas import tpu as pltpu
from jax.sharding import PartitionSpec as P

AXES = ("aa", "ba")
SIDE = 4
DEPTH = 16
FIRSTS, SECONDS = 16, 32
TILE = 256


def flat(x, y, z, core):
    z_hi, z_lo = divmod(z % DEPTH, SIDE)
    return (((x % SIDE) * SIDE + z_lo) * 2 + core) * DEPTH + (y % SIDE) * SIDE + z_hi


def everywhere():
    return [
        (x, y, z, core)
        for x in range(SIDE) for y in range(SIDE) for z in range(DEPTH) for core in range(2)
    ]


def z_groups():
    return [
        [flat(x, y, z, core) for z in range(DEPTH)]
        for x in range(SIDE) for y in range(SIDE) for core in range(2)
    ]


def plane_groups(x_core):
    return [
        [flat(i, u, z, core) if core == x_core else flat(u, i, z, core) for i in range(SIDE)]
        for u in range(SIDE) for z in range(DEPTH) for core in range(2)
    ]


def core_swap():
    return [(flat(x, y, z, core), flat(x, y, z, 1 - core)) for x, y, z, core in everywhere()]


def line_kernel(in_ref, out_ref):
    low = lax.broadcasted_iota(jnp.int32, (32, 128), 1) < 64
    for z_hi in range(SIDE):
        for half in range(2):
            first = in_ref[z_hi * SIDE + 2 * half]
            second = in_ref[z_hi * SIDE + 2 * half + 1]
            upper = jnp.where(low, first, pltpu.roll(second, 64, 1))
            lower = jnp.where(low, pltpu.roll(first, 64, 1), second)
            row, column = z_hi * 64, half * 128
            for copy in range(SIDE):
                out_ref[copy, row : row + 32, column : column + 128] = upper
                out_ref[copy, row + 32 : row + 64, column : column + 128] = lower


def repeat_kernel(in_ref, out_ref):
    for copy in range(SIDE):
        out_ref[copy] = in_ref[...]


def multiply(ints, amps):
    return lax.dot_general(ints, amps, (((1,), (1,)), ((), ())), preferred_element_type=jnp.float32)


def begin_kernel(virt_ref, raw_ref, pair_ref, mine_ref, ints_ref, scale_ref, total_ref):
    rows = raw_ref.shape[0]
    low = lax.broadcasted_iota(jnp.int32, (rows, 128), 1) < 64
    for x in range(SIDE):
        for half in range(2):
            column = x * 512 + half * 256
            first = raw_ref[:, column : column + 128]
            second = raw_ref[:, column + 128 : column + 256]
            to = slice(x * TILE + half * 128, x * TILE + half * 128 + 128)
            ints_ref[0, :, to] = jnp.where(low, first, pltpu.roll(second, 64, 1))
            ints_ref[1, :, to] = jnp.where(low, pltpu.roll(first, 64, 1), second)
    first_at, second_at = lax.axis_index("aa") * FIRSTS, lax.axis_index("ba") * SECONDS
    row = lax.broadcasted_iota(jnp.int32, (SECONDS, TILE), 0)
    seconds = jnp.zeros((SECONDS, TILE), jnp.float32)
    for b in range(SECONDS):
        seconds = jnp.where(row == b, virt_ref[second_at + b], seconds)
    for y in range(SIDE):
        to = slice(y * TILE, y * TILE + TILE)
        pair = pair_ref[:, to]
        for a in range(FIRSTS):
            denominator = virt_ref[first_at + a] + seconds + pair
            scale_ref[a * SECONDS : (a + 1) * SECONDS, to] = 1.0 / denominator
    core = lax.rem(lax.axis_index("aa"), 2)

    def put(y, product):
        total_ref[:, y * TILE : y * TILE + TILE] = product

    add_half(core, ints_ref, mine_ref, put)


def add_half(core, ints_ref, amps_ref, put):
    for of_core in range(2):
        @pl.when(core == of_core)
        def _():
            for y in range(SIDE):
                tiles = [amps_ref[y, x] if of_core == 0 else amps_ref[x, y] for x in range(SIDE)]
                put(y, multiply(ints_ref[of_core], jnp.concatenate(tiles, axis=1)))


def end_kernel(ints_ref, other_ref, scale_ref, start_ref, out_ref):
    core = 1 - lax.rem(lax.axis_index("aa"), 2)

    def put(y, product):
        to = slice(y * TILE, y * TILE + TILE)
        out_ref[:, to] = (start_ref[:, to] + product) * scale_ref[:, to]

    add_half(core, ints_ref, other_ref, put)


SMEM = pl.BlockSpec(memory_space=pltpu.SMEM)
VMEM = pl.BlockSpec(memory_space=pltpu.VMEM)


def call(kernel, ins, outs, specs=None, scratch=(), tiles=0, megabytes=16):
    return pl.pallas_call(
        kernel,
        out_shape=outs,
        in_specs=specs or [VMEM] * len(ins),
        out_specs=jax.tree.map(lambda _: VMEM, outs),
        scratch_shapes=list(scratch),
        compiler_params=pltpu.CompilerParams(vmem_limit_bytes=megabytes * 2**20),
        cost_estimate=pl.CostEstimate(
            flops=tiles * 2 * 512 * TILE * TILE, bytes_accessed=2**18, transcendentals=0
        ),
    )(*ins)


def bf16(*shape):
    return jax.ShapeDtypeStruct(shape, jnp.bfloat16)


def on_device(amplitudes, integrals, virt_energy, pair_energy):
    first_count, second_count, cd_count = integrals.shape
    rows, pairs = first_count * second_count, pair_energy.shape[0]

    packed = jnp.concatenate([amplitudes[:32], amplitudes[32:]], axis=1)
    sent = jnp.broadcast_to(packed[None], (DEPTH, 32, 128))
    lines = lax.all_to_all(sent, AXES, 0, 0, axis_index_groups=z_groups(), tiled=True)
    sent = call(line_kernel, (lines,), bf16(SIDE, TILE, TILE), megabytes=4)
    mine = lax.all_to_all(sent, AXES, 0, 0, axis_index_groups=plane_groups(0), tiled=True)

    mine = call(repeat_kernel, (mine,), bf16(SIDE, SIDE, TILE, TILE), megabytes=6)
    mine = lax.all_to_all(mine, AXES, 0, 0, axis_index_groups=plane_groups(1), tiled=True)
    other = lax.ppermute(mine, AXES, core_swap())
    totals = jax.ShapeDtypeStruct((rows, pairs), jnp.float32)
    ints, scale, total = call(
        begin_kernel,
        (virt_energy, integrals.reshape(rows, cd_count), pair_energy.reshape(1, -1), mine),
        (bf16(2, rows, SIDE * TILE), totals, totals),
        specs=[SMEM, VMEM, VMEM, VMEM], tiles=16,
    )
    update = call(end_kernel, (ints, other, scale, total), totals, tiles=16)
    return update.reshape(first_count, second_count, pairs)


def solution(mesh):
    placed = (P("ba", "aa"), P("aa", "ba", None), P(), P())
    return jax.shard_map(
        on_device, mesh=mesh, in_specs=placed, out_specs=P("aa", "ba", None), check_vma=False
    )
```

```python
import jax
import jax.numpy as jnp
from jax import lax
from jax.experimental import pallas as pl
from jax.experimental.pallas import tpu as pltpu
from jax.sharding import PartitionSpec as P

AXES = ("aa", "ba")
SIDE = 4
DEPTH = 16
FIRSTS, SECONDS = 16, 32
TILE = 256


def flat(x, y, z, core):
    z_hi, z_lo = divmod(z % DEPTH, SIDE)
    return (((x % SIDE) * SIDE + z_lo) * 2 + core) * DEPTH + (y % SIDE) * SIDE + z_hi


def everywhere():
    return [
        (x, y, z, core)
        for x in range(SIDE) for y in range(SIDE) for z in range(DEPTH) for core in range(2)
    ]


def z_groups():
    return [
        [flat(x, y, z, core) for z in range(DEPTH)]
        for x in range(SIDE) for y in range(SIDE) for core in range(2)
    ]


def plane_groups(x_core):
    return [
        [flat(i, u, z, core) if core == x_core else flat(u, i, z, core) for i in range(SIDE)]
        for u in range(SIDE) for z in range(DEPTH) for core in range(2)
    ]


def xy_groups():
    return [
        [flat(x, y, z, core) for y in range(SIDE) for x in range(SIDE)]
        for z in range(DEPTH) for core in range(2)
    ]


def core_swap():
    return [(flat(x, y, z, core), flat(x, y, z, 1 - core)) for x, y, z, core in everywhere()]


def line_kernel(in_ref, out_ref):
    low = lax.broadcasted_iota(jnp.int32, (32, 128), 1) < 64
    for z_hi in range(SIDE):
        for half in range(2):
            first = in_ref[z_hi * SIDE + 2 * half]
            second = in_ref[z_hi * SIDE + 2 * half + 1]
            upper = jnp.where(low, first, pltpu.roll(second, 64, 1))
            lower = jnp.where(low, pltpu.roll(first, 64, 1), second)
            row, column = z_hi * 64, half * 128
            for copy in range(SIDE * SIDE):
                out_ref[copy, row : row + 32, column : column + 128] = upper
                out_ref[copy, row + 32 : row + 64, column : column + 128] = lower


def repeat_kernel(in_ref, out_ref):
    for copy in range(SIDE):
        out_ref[copy] = in_ref[...]


def multiply(ints, amps):
    return lax.dot_general(ints, amps, (((1,), (1,)), ((), ())), preferred_element_type=jnp.float32)


def begin_kernel(virt_ref, raw_ref, pair_ref, mine_ref, ints_ref, scale_ref, total_ref):
    rows = raw_ref.shape[0]
    low = lax.broadcasted_iota(jnp.int32, (rows, 128), 1) < 64
    for x in range(SIDE):
        for half in range(2):
            column = x * 512 + half * 256
            first = raw_ref[:, column : column + 128]
            second = raw_ref[:, column + 128 : column + 256]
            to = slice(x * TILE + half * 128, x * TILE + half * 128 + 128)
            ints_ref[0, :, to] = jnp.where(low, first, pltpu.roll(second, 64, 1))
            ints_ref[1, :, to] = jnp.where(low, pltpu.roll(first, 64, 1), second)
    first_at, second_at = lax.axis_index("aa") * FIRSTS, lax.axis_index("ba") * SECONDS
    row = lax.broadcasted_iota(jnp.int32, (SECONDS, TILE), 0)
    seconds = jnp.zeros((SECONDS, TILE), jnp.float32)
    for b in range(SECONDS):
        seconds = jnp.where(row == b, virt_ref[second_at + b], seconds)
    for y in range(SIDE):
        to = slice(y * TILE, y * TILE + TILE)
        pair = pair_ref[:, to]
        for a in range(FIRSTS):
            denominator = virt_ref[first_at + a] + seconds + pair
            scale_ref[a * SECONDS : (a + 1) * SECONDS, to] = 1.0 / denominator
    core = lax.rem(lax.axis_index("aa"), 2)

    def put(y, product):
        total_ref[:, y * TILE : y * TILE + TILE] = product

    add_half(core, ints_ref, mine_ref, put)


def add_half(core, ints_ref, amps_ref, put):
    for of_core in range(2):
        @pl.when(core == of_core)
        def _():
            for y in range(SIDE):
                tiles = [amps_ref[y, x] for x in range(SIDE)]
                put(y, multiply(ints_ref[of_core], jnp.concatenate(tiles, axis=1)))


def end_kernel(ints_ref, other_ref, scale_ref, start_ref, out_ref, held_ref, sems):
    core = 1 - lax.rem(lax.axis_index("aa"), 2)

    def copy(y):
        to = slice(y * TILE, y * TILE + TILE)
        return pltpu.make_async_copy(held_ref.at[y], out_ref.at[:, to], sems.at[y])

    def put(y, product):
        to = slice(y * TILE, y * TILE + TILE)
        held_ref[y] = (start_ref[:, to] + product) * scale_ref[:, to]
        copy(y).start()

    add_half(core, ints_ref, other_ref, put)
    for y in range(SIDE):
        copy(y).wait()


SMEM = pl.BlockSpec(memory_space=pltpu.SMEM)
VMEM = pl.BlockSpec(memory_space=pltpu.VMEM)


def call(kernel, ins, outs, specs=None, scratch=(), tiles=0, megabytes=16, out_space=pltpu.VMEM):
    return pl.pallas_call(
        kernel,
        out_shape=outs,
        in_specs=specs or [VMEM] * len(ins),
        out_specs=jax.tree.map(lambda _: pl.BlockSpec(memory_space=out_space), outs),
        scratch_shapes=list(scratch),
        compiler_params=pltpu.CompilerParams(vmem_limit_bytes=megabytes * 2**20),
        cost_estimate=pl.CostEstimate(
            flops=tiles * 2 * 512 * TILE * TILE, bytes_accessed=2**18, transcendentals=0
        ),
    )(*ins)


def bf16(*shape):
    return jax.ShapeDtypeStruct(shape, jnp.bfloat16)


def on_device(amplitudes, integrals, virt_energy, pair_energy):
    first_count, second_count, cd_count = integrals.shape
    rows, pairs = first_count * second_count, pair_energy.shape[0]

    packed = jnp.concatenate([amplitudes[:32], amplitudes[32:]], axis=1)
    sent = jnp.broadcast_to(packed[None], (DEPTH, 32, 128))
    lines = lax.all_to_all(sent, AXES, 0, 0, axis_index_groups=z_groups(), tiled=True)
    sent = call(line_kernel, (lines,), bf16(SIDE * SIDE, TILE, TILE), megabytes=4)
    mine = lax.all_to_all(sent, AXES, 0, 0, axis_index_groups=xy_groups(), tiled=True)
    mine = mine.reshape(SIDE, SIDE, TILE, TILE)
    other = lax.ppermute(mine, AXES, core_swap())
    totals = jax.ShapeDtypeStruct((rows, pairs), jnp.float32)
    ints, scale, total = call(
        begin_kernel,
        (virt_energy, integrals.reshape(rows, cd_count), pair_energy.reshape(1, -1), mine),
        (bf16(2, rows, SIDE * TILE), totals, totals),
        specs=[SMEM, VMEM, VMEM, VMEM], tiles=16,
    )
    update = call(
        end_kernel, (ints, other, scale, total), totals, tiles=16, out_space=pl.ANY,
        scratch=[pltpu.VMEM((SIDE, rows, TILE), jnp.float32), pltpu.SemaphoreType.DMA((SIDE,))],
    )
    return update.reshape(first_count, second_count, pairs)


def solution(mesh):
    placed = (P("ba", "aa"), P("aa", "ba", None), P(), P())
    return jax.shard_map(
        on_device, mesh=mesh, in_specs=placed, out_specs=P("aa", "ba", None), check_vma=False
    )
```

```python
import jax
import jax.numpy as jnp
from jax import lax
from jax.experimental import pallas as pl
from jax.experimental.pallas import tpu as pltpu
from jax.sharding import PartitionSpec as P

AXES = ("aa", "ba")
SIDE = 4
DEPTH = 16
PLANE = [2, 3, 0, 1]
ORDER = [10, 11, 12, 13, 14, 15, 0, 1, 2, 3, 4, 5, 6, 7, 8, 9]
FIRSTS, SECONDS = 16, 32
TILE = 256


def flat(x, y, z, core):
    z_hi, z_lo = divmod(z % DEPTH, SIDE)
    return (((x % SIDE) * SIDE + z_lo) * 2 + core) * DEPTH + (y % SIDE) * SIDE + z_hi


def everywhere():
    return [
        (x, y, z, core)
        for x in range(SIDE) for y in range(SIDE) for z in range(DEPTH) for core in range(2)
    ]


def z_groups():
    return [
        [flat(x, y, z, core) for z in ORDER]
        for x in range(SIDE) for y in range(SIDE) for core in range(2)
    ]


def plane_groups(x_core):
    return [
        [flat(i, u, z, core) if core == x_core else flat(u, i, z, core) for i in PLANE]
        for u in range(SIDE) for z in range(DEPTH) for core in range(2)
    ]


def core_swap():
    return [(flat(x, y, z, core), flat(x, y, z, 1 - core)) for x, y, z, core in everywhere()]


def line_kernel(in_ref, out_ref):
    low = lax.broadcasted_iota(jnp.int32, (32, 128), 1) < 64
    for z_hi in range(SIDE):
        for half in range(2):
            first = in_ref[ORDER.index(z_hi * SIDE + 2 * half)]
            second = in_ref[ORDER.index(z_hi * SIDE + 2 * half + 1)]
            upper = jnp.where(low, first, pltpu.roll(second, 64, 1))
            lower = jnp.where(low, pltpu.roll(first, 64, 1), second)
            row, column = z_hi * 64, half * 128
            for copy in range(SIDE):
                out_ref[copy, row : row + 32, column : column + 128] = upper
                out_ref[copy, row + 32 : row + 64, column : column + 128] = lower


def repeat_kernel(in_ref, out_ref):
    for copy in range(SIDE):
        out_ref[copy] = in_ref[...]


def multiply(ints, amps):
    return lax.dot_general(ints, amps, (((1,), (1,)), ((), ())), preferred_element_type=jnp.float32)


def begin_kernel(virt_ref, raw_ref, pair_ref, mine_ref, ints_ref, scale_ref, total_ref):
    rows = raw_ref.shape[0]
    low = lax.broadcasted_iota(jnp.int32, (rows, 128), 1) < 64
    for x in range(SIDE):
        for half in range(2):
            column = x * 512 + half * 256
            first = raw_ref[:, column : column + 128]
            second = raw_ref[:, column + 128 : column + 256]
            to = slice(x * TILE + half * 128, x * TILE + half * 128 + 128)
            ints_ref[0, :, to] = jnp.where(low, first, pltpu.roll(second, 64, 1))
            ints_ref[1, :, to] = jnp.where(low, pltpu.roll(first, 64, 1), second)
    first_at, second_at = lax.axis_index("aa") * FIRSTS, lax.axis_index("ba") * SECONDS
    row = lax.broadcasted_iota(jnp.int32, (SECONDS, TILE), 0)
    seconds = jnp.zeros((SECONDS, TILE), jnp.float32)
    for b in range(SECONDS):
        seconds = jnp.where(row == b, virt_ref[second_at + b], seconds)
    for y in range(SIDE):
        to = slice(y * TILE, y * TILE + TILE)
        pair = pair_ref[:, to]
        for a in range(FIRSTS):
            denominator = virt_ref[first_at + a] + seconds + pair
            scale_ref[a * SECONDS : (a + 1) * SECONDS, to] = 1.0 / denominator
    core = lax.rem(lax.axis_index("aa"), 2)

    def put(y, product):
        total_ref[:, y * TILE : y * TILE + TILE] = product

    add_half(core, ints_ref, mine_ref, put)


def add_half(core, ints_ref, amps_ref, put):
    for of_core in range(2):
        @pl.when(core == of_core)
        def _():
            for y in range(SIDE):
                tiles = [amps_ref[PLANE.index(y), PLANE.index(x)] if of_core == 0 else amps_ref[PLANE.index(x), PLANE.index(y)] for x in range(SIDE)]
                put(y, multiply(ints_ref[of_core], jnp.concatenate(tiles, axis=1)))


def end_kernel(ints_ref, other_ref, scale_ref, start_ref, out_ref, held_ref, sems):
    core = 1 - lax.rem(lax.axis_index("aa"), 2)

    def copy(y):
        to = slice(y * TILE, y * TILE + TILE)
        return pltpu.make_async_copy(held_ref.at[y], out_ref.at[:, to], sems.at[y])

    def put(y, product):
        to = slice(y * TILE, y * TILE + TILE)
        held_ref[y] = (start_ref[:, to] + product) * scale_ref[:, to]
        copy(y).start()

    add_half(core, ints_ref, other_ref, put)
    for y in range(SIDE):
        copy(y).wait()


SMEM = pl.BlockSpec(memory_space=pltpu.SMEM)
VMEM = pl.BlockSpec(memory_space=pltpu.VMEM)


def call(kernel, ins, outs, specs=None, scratch=(), tiles=0, megabytes=16, out_space=pltpu.VMEM):
    return pl.pallas_call(
        kernel,
        out_shape=outs,
        in_specs=specs or [VMEM] * len(ins),
        out_specs=jax.tree.map(lambda _: pl.BlockSpec(memory_space=out_space), outs),
        scratch_shapes=list(scratch),
        compiler_params=pltpu.CompilerParams(vmem_limit_bytes=megabytes * 2**20),
        cost_estimate=pl.CostEstimate(
            flops=tiles * 2 * 512 * TILE * TILE, bytes_accessed=2**18, transcendentals=0
        ),
    )(*ins)


def bf16(*shape):
    return jax.ShapeDtypeStruct(shape, jnp.bfloat16)


def on_device(amplitudes, integrals, virt_energy, pair_energy):
    first_count, second_count, cd_count = integrals.shape
    rows, pairs = first_count * second_count, pair_energy.shape[0]

    packed = jnp.concatenate([amplitudes[:32], amplitudes[32:]], axis=1)
    sent = jnp.broadcast_to(packed[None], (DEPTH, 32, 128))
    lines = lax.all_to_all(sent, AXES, 0, 0, axis_index_groups=z_groups(), tiled=True)
    sent = call(line_kernel, (lines,), bf16(SIDE, TILE, TILE), megabytes=4)
    mine = lax.all_to_all(sent, AXES, 0, 0, axis_index_groups=plane_groups(0), tiled=True)

    mine = call(repeat_kernel, (mine,), bf16(SIDE, SIDE, TILE, TILE), megabytes=6)
    mine = lax.all_to_all(mine, AXES, 0, 0, axis_index_groups=plane_groups(1), tiled=True)
    other = lax.ppermute(mine, AXES, core_swap())
    totals = jax.ShapeDtypeStruct((rows, pairs), jnp.float32)
    ints, scale, total = call(
        begin_kernel,
        (virt_energy, integrals.reshape(rows, cd_count), pair_energy.reshape(1, -1), mine),
        (bf16(2, rows, SIDE * TILE), totals, totals),
        specs=[SMEM, VMEM, VMEM, VMEM], tiles=16,
    )
    update = call(
        end_kernel, (ints, other, scale, total), totals, tiles=16, out_space=pl.ANY,
        scratch=[pltpu.VMEM((SIDE, rows, TILE), jnp.float32), pltpu.SemaphoreType.DMA((SIDE,))],
    )
    return update.reshape(first_count, second_count, pairs)


def solution(mesh):
    placed = (P("ba", "aa"), P("aa", "ba", None), P(), P())
    return jax.shard_map(
        on_device, mesh=mesh, in_specs=placed, out_specs=P("aa", "ba", None), check_vma=False
    )
```

```python
import jax
import jax.numpy as jnp
from jax import lax
from jax.experimental import pallas as pl
from jax.experimental.pallas import tpu as pltpu
from jax.sharding import PartitionSpec as P

AXES = ("aa", "ba")
SIDE = 4
DEPTH = 16
PLANE = [2, 3, 0, 1]
ORDER = [12, 13, 14, 15, 0, 1, 2, 3, 4, 5, 6, 7, 8, 9, 10, 11]
FIRSTS, SECONDS = 16, 32
TILE = 256


def flat(x, y, z, core):
    z_hi, z_lo = divmod(z % DEPTH, SIDE)
    return (((x % SIDE) * SIDE + z_lo) * 2 + core) * DEPTH + (y % SIDE) * SIDE + z_hi


def everywhere():
    return [
        (x, y, z, core)
        for x in range(SIDE) for y in range(SIDE) for z in range(DEPTH) for core in range(2)
    ]


def z_groups():
    return [
        [flat(x, y, z, core) for z in ORDER]
        for x in range(SIDE) for y in range(SIDE) for core in range(2)
    ]


def plane_groups(x_core):
    return [
        [flat(i, u, z, core) if core == x_core else flat(u, i, z, core) for i in PLANE]
        for u in range(SIDE) for z in range(DEPTH) for core in range(2)
    ]


def core_swap():
    return [(flat(x, y, z, core), flat(x, y, z, 1 - core)) for x, y, z, core in everywhere()]


def line_kernel(in_ref, out_ref):
    low = lax.broadcasted_iota(jnp.int32, (32, 128), 1) < 64
    for z_hi in range(SIDE):
        for half in range(2):
            first = in_ref[ORDER.index(z_hi * SIDE + 2 * half)]
            second = in_ref[ORDER.index(z_hi * SIDE + 2 * half + 1)]
            upper = jnp.where(low, first, pltpu.roll(second, 64, 1))
            lower = jnp.where(low, pltpu.roll(first, 64, 1), second)
            row, column = z_hi * 64, half * 128
            for copy in range(SIDE):
                out_ref[copy, row : row + 32, column : column + 128] = upper
                out_ref[copy, row + 32 : row + 64, column : column + 128] = lower


def repeat_kernel(in_ref, out_ref):
    for copy in range(SIDE):
        out_ref[copy] = in_ref[...]


def multiply(ints, amps):
    return lax.dot_general(ints, amps, (((1,), (1,)), ((), ())), preferred_element_type=jnp.float32)


def begin_kernel(virt_ref, raw_ref, pair_ref, mine_ref, ints_ref, scale_ref, total_ref):
    rows = raw_ref.shape[0]
    low = lax.broadcasted_iota(jnp.int32, (rows, 128), 1) < 64
    for x in range(SIDE):
        for half in range(2):
            column = x * 512 + half * 256
            first = raw_ref[:, column : column + 128]
            second = raw_ref[:, column + 128 : column + 256]
            to = slice(x * TILE + half * 128, x * TILE + half * 128 + 128)
            ints_ref[0, :, to] = jnp.where(low, first, pltpu.roll(second, 64, 1))
            ints_ref[1, :, to] = jnp.where(low, pltpu.roll(first, 64, 1), second)
    first_at, second_at = lax.axis_index("aa") * FIRSTS, lax.axis_index("ba") * SECONDS
    row = lax.broadcasted_iota(jnp.int32, (SECONDS, TILE), 0)
    seconds = jnp.zeros((SECONDS, TILE), jnp.float32)
    for b in range(SECONDS):
        seconds = jnp.where(row == b, virt_ref[second_at + b], seconds)
    for y in range(SIDE):
        to = slice(y * TILE, y * TILE + TILE)
        pair = pair_ref[:, to]
        for a in range(FIRSTS):
            denominator = virt_ref[first_at + a] + seconds + pair
            scale_ref[a * SECONDS : (a + 1) * SECONDS, to] = 1.0 / denominator
    core = lax.rem(lax.axis_index("aa"), 2)

    def put(y, product):
        total_ref[:, y * TILE : y * TILE + TILE] = product

    add_half(core, ints_ref, mine_ref, put)


def add_half(core, ints_ref, amps_ref, put):
    for of_core in range(2):
        @pl.when(core == of_core)
        def _():
            for y in range(SIDE):
                tiles = [amps_ref[PLANE.index(y), PLANE.index(x)] if of_core == 0 else amps_ref[PLANE.index(x), PLANE.index(y)] for x in range(SIDE)]
                put(y, multiply(ints_ref[of_core], jnp.concatenate(tiles, axis=1)))


def end_kernel(ints_ref, other_ref, scale_ref, start_ref, out_ref, held_ref, sems):
    core = 1 - lax.rem(lax.axis_index("aa"), 2)

    def copy(y):
        to = slice(y * TILE, y * TILE + TILE)
        return pltpu.make_async_copy(held_ref.at[y], out_ref.at[:, to], sems.at[y])

    def put(y, product):
        to = slice(y * TILE, y * TILE + TILE)
        held_ref[y] = (start_ref[:, to] + product) * scale_ref[:, to]
        copy(y).start()

    add_half(core, ints_ref, other_ref, put)
    for y in range(SIDE):
        copy(y).wait()


SMEM = pl.BlockSpec(memory_space=pltpu.SMEM)
VMEM = pl.BlockSpec(memory_space=pltpu.VMEM)


def call(kernel, ins, outs, specs=None, scratch=(), tiles=0, megabytes=16, out_space=pltpu.VMEM):
    return pl.pallas_call(
        kernel,
        out_shape=outs,
        in_specs=specs or [VMEM] * len(ins),
        out_specs=jax.tree.map(lambda _: pl.BlockSpec(memory_space=out_space), outs),
        scratch_shapes=list(scratch),
        compiler_params=pltpu.CompilerParams(vmem_limit_bytes=megabytes * 2**20),
        cost_estimate=pl.CostEstimate(
            flops=tiles * 2 * 512 * TILE * TILE, bytes_accessed=2**18, transcendentals=0
        ),
    )(*ins)


def bf16(*shape):
    return jax.ShapeDtypeStruct(shape, jnp.bfloat16)


def on_device(amplitudes, integrals, virt_energy, pair_energy):
    first_count, second_count, cd_count = integrals.shape
    rows, pairs = first_count * second_count, pair_energy.shape[0]

    packed = jnp.concatenate([amplitudes[:32], amplitudes[32:]], axis=1)
    sent = jnp.broadcast_to(packed[None], (DEPTH, 32, 128))
    lines = lax.all_to_all(sent, AXES, 0, 0, axis_index_groups=z_groups(), tiled=True)
    sent = call(line_kernel, (lines,), bf16(SIDE, TILE, TILE), megabytes=4)
    mine = lax.all_to_all(sent, AXES, 0, 0, axis_index_groups=plane_groups(0), tiled=True)

    mine = call(repeat_kernel, (mine,), bf16(SIDE, SIDE, TILE, TILE), megabytes=6)
    mine = lax.all_to_all(mine, AXES, 0, 0, axis_index_groups=plane_groups(1), tiled=True)
    other = lax.ppermute(mine, AXES, core_swap())
    totals = jax.ShapeDtypeStruct((rows, pairs), jnp.float32)
    ints, scale, total = call(
        begin_kernel,
        (virt_energy, integrals.reshape(rows, cd_count), pair_energy.reshape(1, -1), mine),
        (bf16(2, rows, SIDE * TILE), totals, totals),
        specs=[SMEM, VMEM, VMEM, VMEM], tiles=16,
    )
    update = call(
        end_kernel, (ints, other, scale, total), totals, tiles=16, out_space=pl.ANY,
        scratch=[pltpu.VMEM((SIDE, rows, TILE), jnp.float32), pltpu.SemaphoreType.DMA((SIDE,))],
    )
    return update.reshape(first_count, second_count, pairs)


def solution(mesh):
    placed = (P("ba", "aa"), P("aa", "ba", None), P(), P())
    return jax.shard_map(
        on_device, mesh=mesh, in_specs=placed, out_specs=P("aa", "ba", None), check_vma=False
    )
```
